32 devices in a mesh: dp: 2 (over core), expert: 16 (over z, y, x).
Axes of the slice: x: 2, y: 2, z: 4, core: 2. Of those that a mesh axis runs over, the one named last changes fastest.
Arguments:
- tokens: bfloat16 [4096, 4096], P(('dp', 'expert')), may hold values from -6 to 6
- cotangent: bfloat16 [4096, 4096], P(('dp', 'expert')), may hold values from -6 to 6
- expert_ids: int32 [4096, 8], P(('dp', 'expert')), may hold values from 0 to 15, all different within a row; in each aligned block of 128 rows (0 to 127, 128 to 255, ...) at most 72 rows name the same one
- route_weight: float32 [4096, 8], P(('dp', 'expert')), may hold values from 0.02 to 0.5
- up_weight: bfloat16 [16, 4096, 768], P('expert'), may hold values from -0.09375 to 0.09375
- down_weight: bfloat16 [16, 768, 4096], P('expert'), may hold values from -0.21875 to 0.21875
Outputs:
- token_grad: bfloat16 [4096, 4096], P(('dp', 'expert'))
- up_grad: float32 [16, 4096, 768], P('expert', 'dp')
- down_grad: float32 [16, 768, 4096], P('expert', 'dp')
The draws below stay inside these ranges and needn't reach their ends.
Inputs may be any that keep to these rules, and one draw needn't show every extreme that they name: `expert_ids`: each row names 8 different experts. Among the 128 tokens of one device (aligned blocks) no expert is named more than 72 times, a bound that some block reaches.
All inputs are finite; a program needn't handle non-finite values.
Results may differ from the reference program's by a relative error of at most 0.017.
Values may be sent and summed in bfloat16 or wider, within the bound.
A program may use at most 192 MiB of HBM per device.

```python
import math
import jax
import jax.numpy as jnp
import numpy as np
from jax import lax

D = 4096
H = 768
TOP = 8
TOK_DEV = 128
EXPERTS = 16
CAP = 72
TOKENS = 4096
N_DP = 2
N_EXPERT = 16


def strengthened(values, own_key, source, target, blocks, factor):
    def block_of(dim):
        return (jnp.arange(values.shape[dim]) // (values.shape[dim] // blocks)).reshape((-1,) + (1,) * (values.ndim - 1 - dim))

    near = jax.random.permutation(own_key, blocks)[block_of(target)]
    other_side = (block_of(target) + blocks // 2) % blocks
    return jnp.where((block_of(source) == near) | (block_of(source) == other_side), factor * values, values)


def block_scale(rng, dims, split, least, largest):
    def one(position, blocks):
        steps = jax.random.uniform(jax.random.fold_in(jax.random.fold_in(rng, 6), position), (blocks,), jnp.float32, least / len(split), largest / len(split))
        return jnp.repeat(jnp.exp(steps), dims[position] // blocks).reshape((-1,) + (1,) * (len(dims) - position - 1))

    level = one(*split[0])
    for cut in split[1:]:
        level = level * one(*cut)
    return level


def shared_out(stream_key, own, number, rows, count, top, bound, skew):
    order = jax.random.permutation(stream_key, count)
    heavy_load, common = shares(count, rows * top, bound, skew, True), shares(count, rows * top, bound, skew, False)
    places = jnp.arange(count)

    def named(lengths, turn):
        used = int((lengths > 0).sum())
        fixed = max(1, used // 4)
        shifted = fixed + (places - fixed + turn * (used - fixed)) % max(1, count - fixed)
        return jnp.zeros((count,), jnp.int32).at[order[jnp.where(places < fixed, places, shifted)]].set(jnp.asarray(lengths, jnp.int32))

    lengths = jnp.where(number % 4 == 0, named(heavy_load, number // 4), named(common, number - number // 4 - 1))
    mixed = jax.random.permutation(jax.random.fold_in(own, 3), count)
    giver, taker = mixed[0:count // 2 * 2:2], mixed[1:count // 2 * 2:2]
    slack = jnp.minimum(lengths[giver] - 1, bound - lengths[taker]) // 2
    slack = jnp.where((giver == order[0]) | (taker == order[0]) | (lengths[taker] == 0), 0, jnp.maximum(slack, 0))
    shifted = jax.random.randint(jax.random.fold_in(own, 4), (count // 2,), 0, 1 << 20) % (slack + 1)
    lengths = lengths.at[giver].add(-shifted).at[taker].add(shifted)
    labels = jnp.searchsorted(jnp.cumsum(lengths), jnp.arange(rows * top), side="right").astype(jnp.int32)
    table = labels.reshape(top, rows).T
    table = table[jax.random.permutation(jax.random.fold_in(own, 1), rows)]
    turn = jax.random.randint(jax.random.fold_in(own, 2), (rows, 1), 0, top)
    return jnp.take_along_axis(table, (jnp.arange(top)[None, :] + turn) % top, axis=1)


def shares(count, total, bound, skew, full):
    loads = [(1 << 20) // math.isqrt(grade ** skew) + 1 for grade in range(1, count + 1)]
    largest = bound if full else min(bound, max(-(-total // count), total * loads[0] // sum(loads)))
    least = 1 if total - largest >= count - 1 else 0
    given, surplus = [largest] + [least] * (count - 1), total - largest - least * (count - 1)
    while surplus > 0:
        free = [i for i in range(1, count) if given[i] < largest] or [i for i in range(1, count) if given[i] < bound]
        whole, left = sum([loads[i] for i in free]), surplus
        for i in free:
            addition = min(bound - given[i], max(1, left * loads[i] // whole), surplus)
            given[i] = given[i] + addition
            surplus = surplus - addition
    return np.array(given)


def normal_values(key, shape, deviation, bound, shards=(), held_as=jnp.bfloat16):
    level = block_scale(key, shape, shards, -0.22, 0.18) if shards else 1.0
    entries = jax.random.normal(key, shape, jnp.float32) * deviation * level
    return jnp.minimum(jnp.maximum(entries, -bound), bound).astype(held_as)


def bell_draw_with(stream_key, shape, scale, bound, pieces, heavy, kind=jnp.bfloat16):
    entries = scale * jax.random.normal(stream_key, shape, jnp.float32)
    if pieces:
        entries = entries * block_scale(stream_key, shape, pieces, -0.22, 0.18)
    return jnp.clip(strengthened(entries, jax.random.fold_in(stream_key, 3), *heavy), -bound, bound).astype(kind)


def setup_inputs(seed: int = 0) -> dict:
    key_list = jax.random.split(jax.random.key(seed), 7)
    tokens = bell_draw_with(key_list[0], (TOKENS, D), 1.0, 6.0, ((0, 32),), (0, 1, 32, 2.75))
    cotangent = normal_values(key_list[1], (TOKENS, D), 1.0, 6.0, ((0, 32),))
    expert_ids_keys = jax.random.split(jax.random.fold_in(key_list[2], 1), TOKENS // TOK_DEV)
    expert_ids_turns = jax.random.permutation(jax.random.fold_in(key_list[2], 3), TOKENS // TOK_DEV)
    expert_ids = jax.vmap(lambda own, number: shared_out(jax.random.fold_in(key_list[2], 2), own, number, TOK_DEV, EXPERTS, TOP, CAP, 1))(expert_ids_keys, expert_ids_turns).reshape((TOKENS, TOP))
    route_weight = jnp.clip(jnp.exp(math.log(0.5) - 3.218876 * jax.random.uniform(key_list[3], (TOKENS, TOP), jnp.float32) ** block_scale(key_list[3], (TOKENS, TOP), ((0, 32),), -0.2, 0.2)), 0.02, 0.5)
    up_weight = normal_values(key_list[4], (EXPERTS, D, H), D ** -0.5, 0.09375, ((0, 16),))
    down_weight = normal_values(key_list[5], (EXPERTS, H, D), H ** -0.5, 0.21875, ((0, 16),))
    return dict(tokens=tokens, cotangent=cotangent, expert_ids=expert_ids, route_weight=route_weight, up_weight=up_weight, down_weight=down_weight)


def reference(tokens, cotangent, expert_ids, route_weight, up_weight, down_weight):
    group_rows = N_EXPERT * TOK_DEV
    slots = N_EXPERT * CAP

    def one_expert(grad_total, expert):
        w_up = up_weight[expert]
        w_down = down_weight[expert]

        def one_group(carry, group):
            grad_acc, up_acc, down_acc = carry
            start = (group * group_rows).astype(jnp.int32)
            ids_group = lax.dynamic_slice_in_dim(expert_ids, start, group_rows, 0)
            present = jnp.any(ids_group == expert, axis=1)
            order = jnp.argsort(jnp.where(present, 0, 1).astype(jnp.int32), stable=True)[:slots].astype(jnp.int32)
            valid = present[order]
            index = (order + start).astype(jnp.int32)
            rows_x = jnp.where(valid[:, None], tokens[index], jnp.zeros((), tokens.dtype)).astype(jnp.bfloat16)
            weight_e = jnp.sum(jnp.where(expert_ids[index] == expert, route_weight[index], jnp.float32(0.0)), axis=1)
            rows_g = (weight_e[:, None] * cotangent[index].astype(jnp.float32)).astype(jnp.bfloat16)
            pre = jnp.dot(rows_x, w_up, preferred_element_type=jnp.float32)
            sigma = jax.nn.sigmoid(pre)
            active = (pre * sigma).astype(jnp.bfloat16)
            back = jnp.dot(rows_g, w_down.T, preferred_element_type=jnp.float32)
            pre_grad = (back * sigma * (1.0 + pre * (1.0 - sigma))).astype(jnp.bfloat16)
            row_grad = jnp.dot(pre_grad, w_up.T, preferred_element_type=jnp.float32).astype(jnp.bfloat16)
            row_grad = lax.optimization_barrier(row_grad).astype(jnp.float32)
            grad_acc = grad_acc.at[index].add(jnp.where(valid[:, None], row_grad, jnp.float32(0.0)))
            up_part = jnp.dot(rows_x.T, pre_grad, preferred_element_type=jnp.float32).astype(jnp.bfloat16)
            down_part = jnp.dot(active.T, rows_g, preferred_element_type=jnp.float32).astype(jnp.bfloat16)
            up_part, down_part = lax.optimization_barrier((up_part, down_part))
            return (grad_acc, up_acc + up_part.astype(jnp.float32), down_acc + down_part.astype(jnp.float32)), None

        start_carry = (grad_total, jnp.zeros((D, H), jnp.float32), jnp.zeros((H, D), jnp.float32))
        (grad_total, up_sum, down_sum), _ = lax.scan(one_group, start_carry, jnp.arange(N_DP, dtype=jnp.int32))
        return grad_total, (up_sum, down_sum)

    grad_start = jnp.zeros((TOKENS, D), jnp.float32)
    grad_total, (up_grad, down_grad) = lax.scan(one_expert, grad_start, jnp.arange(EXPERTS, dtype=jnp.int32))
    return grad_total.astype(jnp.bfloat16), up_grad, down_grad
```

```python
import jax
import jax.numpy as jnp
from jax import lax
from jax.sharding import PartitionSpec as P

CHUNKS = 2


def dot(a, b, dims):
    return lax.dot_general(a, b, (dims, ((), ())), preferred_element_type=jnp.float32)


def body(tokens, cotangent, expert_ids, route_weight, up_weight, down_weight):
    rows, width = tokens.shape
    me = lax.axis_index("expert")
    up_matrix = up_weight[0]
    down_matrix = down_weight[0]
    experts = jnp.arange(lax.axis_size("expert"), dtype=jnp.int32)
    weight = jnp.sum(
        jnp.where(expert_ids[:, :, None] == experts, route_weight[:, :, None], 0.0), axis=1
    )
    weight_all = lax.all_gather(weight, "expert", axis=0, tiled=False)
    mine = lax.dynamic_index_in_dim(weight_all, me, axis=2, keepdims=False)

    step = rows // CHUNKS
    parts = []
    for c in range(CHUNKS):
        x = lax.all_gather(tokens[c * step : (c + 1) * step], "expert", axis=0, tiled=True)
        g = lax.all_gather(cotangent[c * step : (c + 1) * step], "expert", axis=0, tiled=True)
        w = mine[:, c * step : (c + 1) * step].reshape(-1, 1)
        parts.append((x, g, w))

    up_sum = None
    down_sum = None
    grads = []
    for x, g, w in parts:
        pre = dot(x, up_matrix, ((1,), (0,)))
        sigma = jax.nn.sigmoid(pre)
        active = (pre * sigma).astype(jnp.bfloat16)
        scaled = (w * g.astype(jnp.float32)).astype(jnp.bfloat16)
        back = dot(scaled, down_matrix, ((1,), (1,)))
        pre_grad = (back * sigma * (1.0 + pre * (1.0 - sigma))).astype(jnp.bfloat16)
        row_grad = dot(pre_grad, up_matrix, ((1,), (1,))).astype(jnp.bfloat16)
        grads.append(lax.psum_scatter(row_grad, "expert", scatter_dimension=0, tiled=True))
        up_part = dot(x, pre_grad, ((0,), (0,)))
        down_part = dot(active, scaled, ((0,), (0,)))
        up_sum = up_part if up_sum is None else up_sum + up_part
        down_sum = down_part if down_sum is None else down_sum + down_part
    token_grad = jnp.concatenate(grads, axis=0)
    up_grad = lax.psum_scatter(
        up_sum.astype(jnp.bfloat16), "dp", scatter_dimension=0, tiled=True
    ).astype(jnp.float32)
    down_grad = lax.psum_scatter(
        down_sum.astype(jnp.bfloat16), "dp", scatter_dimension=0, tiled=True
    ).astype(jnp.float32)
    return (token_grad, up_grad[None], down_grad[None])


def solution(mesh):
    in_specs = (
        P(("dp", "expert"), None),
        P(("dp", "expert"), None),
        P(("dp", "expert"), None),
        P(("dp", "expert"), None),
        P("expert", None, None),
        P("expert", None, None),
    )
    out_specs = (P(("dp", "expert"), None), P("expert", "dp", None), P("expert", "dp", None))
    return jax.shard_map(body, mesh=mesh, in_specs=in_specs, out_specs=out_specs, check_vma=False)
```

```python
import jax
import jax.numpy as jnp
from jax import lax
from jax.sharding import PartitionSpec as P


def dot(a, b, dims):
    return lax.dot_general(a, b, (dims, ((), ())), preferred_element_type=jnp.float32)


def body(tokens, cotangent, expert_ids, route_weight, up_weight, down_weight):
    groups = lax.axis_size("expert")
    rows, width = tokens.shape
    capacity = rows * expert_ids.shape[1] * 9 // (8 * groups)
    inner = 1 << ((groups.bit_length() - 1) // 2)
    outer = groups // inner
    me = lax.axis_index("expert")
    my_outer, my_inner = me // inner, me % inner
    up_matrix = up_weight[0]
    down_matrix = down_weight[0]

    def from_outer(value, k):
        pairs = [(((o + k) % outer) * inner + i, o * inner + i) for o in range(outer) for i in range(inner)]
        return lax.ppermute(value, "expert", pairs)

    def to_outer(value, k):
        pairs = [(o * inner + i, ((o + k) % outer) * inner + i) for o in range(outer) for i in range(inner)]
        return lax.ppermute(value, "expert", pairs)

    def swap_inner(value, j):
        pairs = [(o * inner + i, o * inner + (i ^ j)) for o in range(outer) for i in range(inner)]
        return lax.ppermute(value, "expert", pairs)

    experts = jnp.arange(groups, dtype=jnp.int32)
    weight = jnp.sum(
        jnp.where(expert_ids[:, :, None] == experts, route_weight[:, :, None], 0.0), axis=1
    )
    weights = [weight] + [from_outer(weight, k) for k in range(1, outer)]
    xs = [tokens] + [from_outer(tokens, k) for k in range(1, outer)]
    gs = [cotangent] + [from_outer(cotangent, k) for k in range(1, outer)]

    before = (jnp.arange(rows)[:, None] > jnp.arange(rows)[None, :]).astype(jnp.bfloat16)
    target = my_outer * inner + (my_inner ^ jnp.arange(inner, dtype=jnp.int32))

    all_x, all_g, all_active, all_pre_grad = [], [], [], []
    total = None
    for k in range(outer):
        chosen = jnp.sum(
            jnp.where(experts[:, None] == target[None, :], weights[k][:, :, None], 0.0), axis=1
        )
        present = chosen > 0.0
        rank = dot(before, present.astype(jnp.bfloat16), ((1,), (0,))).astype(jnp.int32)
        place = jnp.where(present, rank, -1).T
        pick = place[:, None, :] == jnp.arange(capacity, dtype=jnp.int32)[None, :, None]
        packed_weight = jnp.sum(jnp.where(pick, chosen.T[:, None, :], 0.0), axis=2)
        pick = pick.astype(jnp.bfloat16)
        got_x, got_g = [], []
        for j in range(inner):
            x = dot(pick[j], xs[k], ((1,), (0,))).astype(jnp.bfloat16)
            g = (packed_weight[j][:, None] * dot(pick[j], gs[k], ((1,), (0,)))).astype(jnp.bfloat16)
            got_x.append(swap_inner(x, j) if j else x)
            got_g.append(swap_inner(g, j) if j else g)
        x = jnp.concatenate(got_x, axis=0)
        g = jnp.concatenate(got_g, axis=0)
        pre = dot(x, up_matrix, ((1,), (0,)))
        sigma = jax.nn.sigmoid(pre)
        active = (pre * sigma).astype(jnp.bfloat16)
        back = dot(g, down_matrix, ((1,), (1,)))
        pre_grad = (back * sigma * (1.0 + pre * (1.0 - sigma))).astype(jnp.bfloat16)
        row_grad = dot(pre_grad, up_matrix, ((1,), (1,))).astype(jnp.bfloat16)
        returned = []
        for j in range(inner):
            piece = row_grad[j * capacity : (j + 1) * capacity]
            returned.append(swap_inner(piece, j) if j else piece)
        part = dot(pick.reshape(inner * capacity, rows), jnp.concatenate(returned, axis=0), ((0,), (0,)))
        if k:
            part = to_outer(part.astype(jnp.bfloat16), k).astype(jnp.float32)
        total = part if total is None else total + part
        all_x.append(x)
        all_g.append(g)
        all_active.append(active)
        all_pre_grad.append(pre_grad)

    x, g, active, pre_grad = [
        jnp.concatenate(parts, axis=0) for parts in (all_x, all_g, all_active, all_pre_grad)
    ]
    up_grad = lax.psum_scatter(
        dot(x, pre_grad, ((0,), (0,))).astype(jnp.bfloat16), "dp", scatter_dimension=0, tiled=True
    ).astype(jnp.float32)
    down_grad = lax.psum_scatter(
        dot(active, g, ((0,), (0,))).astype(jnp.bfloat16), "dp", scatter_dimension=0, tiled=True
    ).astype(jnp.float32)
    return (total.astype(jnp.bfloat16), up_grad[None], down_grad[None])


def solution(mesh):
    in_specs = (
        P(("dp", "expert"), None),
        P(("dp", "expert"), None),
        P(("dp", "expert"), None),
        P(("dp", "expert"), None),
        P("expert", None, None),
        P("expert", None, None),
    )
    out_specs = (P(("dp", "expert"), None), P("expert", "dp", None), P("expert", "dp", None))
    return jax.shard_map(body, mesh=mesh, in_specs=in_specs, out_specs=out_specs, check_vma=False)
```

```python
import functools

import jax
import jax.numpy as jnp
from jax import lax
from jax.experimental import pallas as pl
from jax.experimental.pallas import tpu as pltpu
from jax.sharding import PartitionSpec as P

CHUNKS = 4
MIB = 1024 * 1024


def dot(a, b, dims):
    return lax.dot_general(a, b, (dims, ((), ())), preferred_element_type=jnp.float32)


def device(o, i, inner):
    return {"expert": o * inner + i}


def greet(outer, inner, o, i):
    barrier = pltpu.get_barrier_semaphore()
    for k in range(1, outer):
        pl.semaphore_signal(
            barrier, inc=1, device_id=device((o + k) % outer, i, inner), device_id_type=pl.DeviceIdType.MESH
        )
    for j in range(1, inner):
        pl.semaphore_signal(
            barrier, inc=1, device_id=device(o, i ^ j, inner), device_id_type=pl.DeviceIdType.MESH
        )
    pl.semaphore_wait(barrier, outer + inner - 2)


def remote(src, dst, send_sem, recv_sem, to):
    return pltpu.make_async_remote_copy(
        src_ref=src, dst_ref=dst, send_sem=send_sem, recv_sem=recv_sem,
        device_id=to, device_id_type=pl.DeviceIdType.MESH,
    )


def dispatch_kernel(outer, inner, x_ref, g_ref, pick_ref, scale_ref, out_x, out_g,
                    land, packed, z_send, z_recv, p_send, p_recv):
    me = lax.axis_index("expert")
    o, i = me // inner, me % inner
    rows = x_ref.shape[0]
    block = pick_ref.shape[0] // inner
    wide = land.shape[2]
    greet(outer, inner, o, i)

    arriving = []
    for n in range(2 * CHUNKS):
        source = (x_ref if n < CHUNKS else g_ref).at[:, pl.ds((n % CHUNKS) * wide, wide)]
        copies = []
        for k in range(outer):
            place = land.at[n, pl.ds(k * rows, rows)]
            if k:
                copy = remote(source, place, z_send.at[n, k], z_recv.at[n, k],
                              device((o + outer - k) % outer, i, inner))
            else:
                copy = pltpu.make_async_copy(source, place, z_recv.at[n, k])
            copy.start()
            copies.append(copy)
        arriving.append(copies)

    leaving = []
    for n in range(2 * CHUNKS):
        for copy in arriving[n]:
            copy.wait()
        result = (out_x if n < CHUNKS else out_g)
        columns = pl.ds((n % CHUNKS) * wide, wide)
        for j in list(range(1, inner)) + [0]:
            span = pl.ds(j * block, block)
            rows_j = dot(pick_ref[span, :], land[n], ((1,), (0,)))
            if n >= CHUNKS:
                rows_j = scale_ref[span, :] * rows_j
            packed[n, span, :] = rows_j.astype(jnp.bfloat16)
            source, place = packed.at[n, span], result.at[span, columns]
            if j:
                copy = remote(source, place, p_send.at[n, j], p_recv.at[n, j], device(o, i ^ j, inner))
            else:
                copy = pltpu.make_async_copy(source, place, p_recv.at[n, j])
            copy.start()
            leaving.append(copy)
    for copy in leaving:
        copy.wait()


def return_kernel(outer, inner, grad_ref, put_ref, out_ref,
                  back, parts, land, total, p_send, p_recv, z_send, z_recv):
    me = lax.axis_index("expert")
    o, i = me // inner, me % inner
    rows = out_ref.shape[0]
    block = put_ref.shape[1] // inner
    wide = back.shape[2]
    greet(outer, inner, o, i)

    arriving = []
    for n in range(CHUNKS):
        copies = []
        for j in range(inner):
            span = pl.ds(j * block, block)
            source, place = grad_ref.at[span, pl.ds(n * wide, wide)], back.at[n, span]
            if j:
                copy = remote(source, place, p_send.at[n, j], p_recv.at[n, j], device(o, i ^ j, inner))
            else:
                copy = pltpu.make_async_copy(source, place, p_recv.at[n, j])
            copy.start()
            copies.append(copy)
        arriving.append(copies)

    leaving = []
    for n in range(CHUNKS):
        for copy in arriving[n]:
            copy.wait()
        copies = []
        for k in list(range(1, outer)) + [0]:
            span = pl.ds(k * rows, rows)
            part = dot(put_ref[span, :], back[n], ((1,), (0,)))
            if k:
                parts[n, span, :] = part.astype(jnp.bfloat16)
                copy = remote(parts.at[n, span], land.at[n, span], z_send.at[n, k], z_recv.at[n, k],
                              device((o + k) % outer, i, inner))
                copy.start()
                copies.append(copy)
            else:
                total[n] = part
        leaving.append(copies)
    for n in range(CHUNKS):
        for copy in leaving[n]:
            copy.wait()
        value = total[n]
        for k in range(1, outer):
            value = value + land[n, pl.ds(k * rows, rows), :].astype(jnp.float32)
        out_ref[:, pl.ds(n * wide, wide)] = value.astype(jnp.bfloat16)


def body(tokens, cotangent, expert_ids, route_weight, up_weight, down_weight):
    groups = lax.axis_size("expert")
    rows, width = tokens.shape
    capacity = rows * expert_ids.shape[1] * 9 // (8 * groups)
    inner = 1 << ((groups.bit_length() - 1) // 2)
    outer = groups // inner
    wide = width // CHUNKS
    slots = inner * outer * capacity
    me = lax.axis_index("expert")
    my_outer, my_inner = me // inner, me % inner
    up_matrix = up_weight[0]
    down_matrix = down_weight[0]

    def from_outer(value, k):
        pairs = [(((o + k) % outer) * inner + i, o * inner + i) for o in range(outer) for i in range(inner)]
        return lax.ppermute(value, "expert", pairs)

    experts = jnp.arange(groups, dtype=jnp.int32)
    weight = jnp.sum(
        jnp.where(expert_ids[:, :, None] == experts, route_weight[:, :, None], 0.0), axis=1
    )
    weights = jnp.stack([weight] + [from_outer(weight, k) for k in range(1, outer)])
    target = my_outer * inner + (my_inner ^ jnp.arange(inner, dtype=jnp.int32))
    chosen = jnp.sum(
        jnp.where(experts[:, None] == target[None, :], weights[:, :, :, None], 0.0), axis=2
    )
    present = chosen > 0.0
    before = (jnp.arange(rows)[:, None] > jnp.arange(rows)[None, :]).astype(jnp.bfloat16)
    rank = jnp.einsum(
        "ut,ktj->jku", before, present.astype(jnp.bfloat16), preferred_element_type=jnp.float32
    ).astype(jnp.int32)
    place = jnp.where(present.transpose(2, 0, 1), rank, -1)
    chosen = chosen.transpose(2, 0, 1)
    slot = jnp.arange(capacity, dtype=jnp.int32)
    own = jnp.eye(outer, dtype=jnp.bool_)
    hit = place[:, :, None, :] == slot[None, None, :, None]
    scale = jnp.sum(jnp.where(hit, chosen[:, :, None, :], 0.0), axis=3).reshape(slots, 1)
    pick = (hit[:, :, :, None, :] & own[None, :, None, :, None]).astype(jnp.bfloat16)
    pick = pick.reshape(slots, outer * rows)
    put = pick.T

    any_space = pl.BlockSpec(memory_space=pl.ANY)
    vmem = pl.BlockSpec(memory_space=pltpu.VMEM)
    dma = pltpu.SemaphoreType.DMA
    flat_x, flat_g = pl.pallas_call(
        functools.partial(dispatch_kernel, outer, inner),
        out_shape=[jax.ShapeDtypeStruct((slots, width), jnp.bfloat16)] * 2,
        in_specs=[any_space, any_space, vmem, vmem],
        out_specs=[any_space, any_space],
        scratch_shapes=[
            pltpu.VMEM((2 * CHUNKS, outer * rows, wide), jnp.bfloat16),
            pltpu.VMEM((2 * CHUNKS, slots, wide), jnp.bfloat16),
            dma((2 * CHUNKS, outer)), dma((2 * CHUNKS, outer)),
            dma((2 * CHUNKS, inner)), dma((2 * CHUNKS, inner)),
        ],
        compiler_params=pltpu.CompilerParams(
            collective_id=0, has_side_effects=True, vmem_limit_bytes=48 * MIB
        ),
        name="dispatch",
    )(tokens, cotangent, pick, scale)

    pre = dot(flat_x, up_matrix, ((1,), (0,)))
    sigma = jax.nn.sigmoid(pre)
    active = (pre * sigma).astype(jnp.bfloat16)
    back = dot(flat_g, down_matrix, ((1,), (1,)))
    pre_grad = (back * sigma * (1.0 + pre * (1.0 - sigma))).astype(jnp.bfloat16)
    row_grad = dot(pre_grad, up_matrix, ((1,), (1,))).astype(jnp.bfloat16)

    token_grad = pl.pallas_call(
        functools.partial(return_kernel, outer, inner),
        out_shape=jax.ShapeDtypeStruct((rows, width), jnp.bfloat16),
        in_specs=[any_space, vmem],
        out_specs=vmem,
        scratch_shapes=[
            pltpu.VMEM((CHUNKS, slots, wide), jnp.bfloat16),
            pltpu.VMEM((CHUNKS, outer * rows, wide), jnp.bfloat16),
            pltpu.VMEM((CHUNKS, outer * rows, wide), jnp.bfloat16),
            pltpu.VMEM((CHUNKS, rows, wide), jnp.float32),
            dma((CHUNKS, inner)), dma((CHUNKS, inner)),
            dma((CHUNKS, outer)), dma((CHUNKS, outer)),
        ],
        compiler_params=pltpu.CompilerParams(
            collective_id=1, has_side_effects=True, vmem_limit_bytes=48 * MIB
        ),
        name="bring_back",
    )(row_grad, put)

    up_grad = lax.psum_scatter(
        dot(flat_x, pre_grad, ((0,), (0,))).astype(jnp.bfloat16), "dp", scatter_dimension=0, tiled=True
    ).astype(jnp.float32)
    down_grad = lax.psum_scatter(
        dot(active, flat_g, ((0,), (0,))).astype(jnp.bfloat16), "dp", scatter_dimension=0, tiled=True
    ).astype(jnp.float32)
    return (token_grad, up_grad[None], down_grad[None])


def solution(mesh):
    in_specs = (
        P(("dp", "expert"), None),
        P(("dp", "expert"), None),
        P(("dp", "expert"), None),
        P(("dp", "expert"), None),
        P("expert", None, None),
        P("expert", None, None),
    )
    out_specs = (P(("dp", "expert"), None), P("expert", "dp", None), P("expert", "dp", None))
    return jax.shard_map(body, mesh=mesh, in_specs=in_specs, out_specs=out_specs, check_vma=False)
```

```python
import functools

import jax
import jax.numpy as jnp
from jax import lax
from jax.experimental import pallas as pl
from jax.experimental.pallas import tpu as pltpu
from jax.sharding import PartitionSpec as P

CHUNKS = 4
AHEAD = 3
MIB = 1024 * 1024


def dot(a, b, dims):
    return lax.dot_general(a, b, (dims, ((), ())), preferred_element_type=jnp.float32)


def device(o, i, inner):
    return {"expert": o * inner + i}


def greet(outer, inner, o, i):
    barrier = pltpu.get_barrier_semaphore()
    for k in range(1, outer):
        pl.semaphore_signal(
            barrier, inc=1, device_id=device((o + k) % outer, i, inner), device_id_type=pl.DeviceIdType.MESH
        )
    for j in range(1, inner):
        pl.semaphore_signal(
            barrier, inc=1, device_id=device(o, i ^ j, inner), device_id_type=pl.DeviceIdType.MESH
        )
    pl.semaphore_wait(barrier, outer + inner - 2)


def remote(src, dst, send_sem, recv_sem, to):
    return pltpu.make_async_remote_copy(
        src_ref=src, dst_ref=dst, send_sem=send_sem, recv_sem=recv_sem,
        device_id=to, device_id_type=pl.DeviceIdType.MESH,
    )


def dispatch_kernel(outer, inner, x_ref, g_ref, pick_ref, scale_ref, out_x, out_g,
                    land, packed, z_send, z_recv, p_send, p_recv):
    me = lax.axis_index("expert")
    o, i = me // inner, me % inner
    rows = x_ref.shape[0]
    block = pick_ref.shape[0] // inner
    wide = land.shape[2]
    greet(outer, inner, o, i)

    def place(n, k):
        return land.at[n, pl.ds(k * rows, rows)]

    def own(n):
        return (x_ref if n < CHUNKS else g_ref).at[:, pl.ds((n % CHUNKS) * wide, wide)]

    def down(n, k):
        return remote(own(n) if k == 0 else place(n, k), place(n, k + 1), z_send.at[n, 0, k],
                      z_recv.at[n, k + 1], device(o - 1, i, inner))

    def up(n, k):
        return remote(own(n) if k == outer else place(n, k), place(n, k - 1), z_send.at[n, 1, k - 1],
                      z_recv.at[n, k - 1], device(o + 1, i, inner))

    def keep(n):
        return pltpu.make_async_copy(own(n), place(n, 0), z_recv.at[n, 0])

    def each_send(n, k, act):
        if k < outer - 1:
            @pl.when((o >= 1) & (o + k < outer))
            def _():
                act(down(n, k))
        if k >= 2:
            @pl.when((o < outer - 1) & (o + k >= outer))
            def _():
                act(up(n, k))

    def start_own(n):
        each_send(n, 0, lambda copy: copy.start())
        each_send(n, outer, lambda copy: copy.start())
        keep(n).start()

    def arrive(n, k):
        pltpu.make_async_copy(place(n, k), place(n, k), z_recv.at[n, k]).wait()
        each_send(n, k, lambda copy: copy.start())

    near = sorted({1, outer - 1} - {0})
    far = [k for k in range(1, outer) if k not in near]
    steps = 2 * CHUNKS
    for n in range(min(AHEAD, steps)):
        start_own(n)
    inside = (o >= 1) & (o < outer - 1)

    def arrive_near(n, when):
        @pl.when(when)
        def _():
            for k in near:
                arrive(n, k)

    arrive_near(0, inside)

    leaving = []
    for n in range(steps):
        if n + AHEAD < steps:
            start_own(n + AHEAD)
        if n + 1 < steps:
            arrive_near(n + 1, inside)
        arrive_near(n, jnp.logical_not(inside))
        for k in far:
            arrive(n, k)
        keep(n).wait()
        result = (out_x if n < CHUNKS else out_g)
        columns = pl.ds((n % CHUNKS) * wide, wide)
        for j in list(range(1, inner)) + [0]:
            span = pl.ds(j * block, block)
            rows_j = dot(pick_ref[span, :], land[n], ((1,), (0,)))
            if n >= CHUNKS:
                rows_j = scale_ref[span, :] * rows_j
            packed[n, span, :] = rows_j.astype(jnp.bfloat16)
            source, goal = packed.at[n, span], result.at[span, columns]
            if j:
                copy = remote(source, goal, p_send.at[n, j], p_recv.at[n, j], device(o, i ^ j, inner))
            else:
                copy = pltpu.make_async_copy(source, goal, p_recv.at[n, j])
            copy.start()
            leaving.append(copy)
    for copy in leaving:
        copy.wait()
    for n in range(steps):
        for k in range(outer + 1):
            each_send(n, k, lambda copy: copy.wait_send())


def return_kernel(outer, inner, grad_ref, put_ref, out_ref,
                  back, parts, land, total, p_send, p_recv, z_send, z_recv):
    me = lax.axis_index("expert")
    o, i = me // inner, me % inner
    rows = out_ref.shape[0]
    block = put_ref.shape[1] // inner
    wide = back.shape[2]
    greet(outer, inner, o, i)

    arriving = []
    for n in range(CHUNKS):
        copies = []
        for j in range(inner):
            span = pl.ds(j * block, block)
            source, place = grad_ref.at[span, pl.ds(n * wide, wide)], back.at[n, span]
            if j:
                copy = remote(source, place, p_send.at[n, j], p_recv.at[n, j], device(o, i ^ j, inner))
            else:
                copy = pltpu.make_async_copy(source, place, p_recv.at[n, j])
            copy.start()
            copies.append(copy)
        arriving.append(copies)

    leaving = []
    for n in range(CHUNKS):
        for copy in arriving[n]:
            copy.wait()
        copies = []
        for k in list(range(1, outer)) + [0]:
            span = pl.ds(k * rows, rows)
            part = dot(put_ref[span, :], back[n], ((1,), (0,)))
            if k:
                parts[n, span, :] = part.astype(jnp.bfloat16)
                copy = remote(parts.at[n, span], land.at[n, span], z_send.at[n, k], z_recv.at[n, k],
                              device((o + k) % outer, i, inner))
                copy.start()
                copies.append(copy)
            else:
                total[n] = part
        leaving.append(copies)
    for n in range(CHUNKS):
        for copy in leaving[n]:
            copy.wait()
        value = total[n]
        for k in range(1, outer):
            value = value + land[n, pl.ds(k * rows, rows), :].astype(jnp.float32)
        out_ref[:, pl.ds(n * wide, wide)] = value.astype(jnp.bfloat16)


def body(tokens, cotangent, expert_ids, route_weight, up_weight, down_weight):
    groups = lax.axis_size("expert")
    rows, width = tokens.shape
    capacity = rows * expert_ids.shape[1] * 9 // (8 * groups)
    inner = 1 << ((groups.bit_length() - 1) // 2)
    outer = groups // inner
    wide = width // CHUNKS
    slots = inner * outer * capacity
    me = lax.axis_index("expert")
    my_outer, my_inner = me // inner, me % inner
    up_matrix = up_weight[0]
    down_matrix = down_weight[0]

    def from_outer(value, k):
        pairs = [(((o + k) % outer) * inner + i, o * inner + i) for o in range(outer) for i in range(inner)]
        return lax.ppermute(value, "expert", pairs)

    experts = jnp.arange(groups, dtype=jnp.int32)
    weight = jnp.sum(
        jnp.where(expert_ids[:, :, None] == experts, route_weight[:, :, None], 0.0), axis=1
    )
    weights = jnp.stack([weight] + [from_outer(weight, k) for k in range(1, outer)])
    target = my_outer * inner + (my_inner ^ jnp.arange(inner, dtype=jnp.int32))
    chosen = jnp.sum(
        jnp.where(experts[:, None] == target[None, :], weights[:, :, :, None], 0.0), axis=2
    )
    present = chosen > 0.0
    before = (jnp.arange(rows)[:, None] > jnp.arange(rows)[None, :]).astype(jnp.bfloat16)
    rank = jnp.einsum(
        "ut,ktj->jku", before, present.astype(jnp.bfloat16), preferred_element_type=jnp.float32
    ).astype(jnp.int32)
    place = jnp.where(present.transpose(2, 0, 1), rank, -1)
    chosen = chosen.transpose(2, 0, 1)
    slot = jnp.arange(capacity, dtype=jnp.int32)
    own = jnp.eye(outer, dtype=jnp.bool_)
    hit = place[:, :, None, :] == slot[None, None, :, None]
    scale = jnp.sum(jnp.where(hit, chosen[:, :, None, :], 0.0), axis=3).reshape(slots, 1)
    pick = (hit[:, :, :, None, :] & own[None, :, None, :, None]).astype(jnp.bfloat16)
    pick = pick.reshape(slots, outer * rows)
    put = pick.T

    any_space = pl.BlockSpec(memory_space=pl.ANY)
    vmem = pl.BlockSpec(memory_space=pltpu.VMEM)
    dma = pltpu.SemaphoreType.DMA
    flat_x, flat_g = pl.pallas_call(
        functools.partial(dispatch_kernel, outer, inner),
        out_shape=[jax.ShapeDtypeStruct((slots, width), jnp.bfloat16)] * 2,
        in_specs=[any_space, any_space, vmem, vmem],
        out_specs=[any_space, any_space],
        scratch_shapes=[
            pltpu.VMEM((2 * CHUNKS, outer * rows, wide), jnp.bfloat16),
            pltpu.VMEM((2 * CHUNKS, slots, wide), jnp.bfloat16),
            dma((2 * CHUNKS, 2, outer)), dma((2 * CHUNKS, outer)),
            dma((2 * CHUNKS, inner)), dma((2 * CHUNKS, inner)),
        ],
        compiler_params=pltpu.CompilerParams(
            collective_id=0, has_side_effects=True, vmem_limit_bytes=48 * MIB
        ),
        name="dispatch",
    )(tokens, cotangent, pick, scale)

    pre = dot(flat_x, up_matrix, ((1,), (0,)))
    sigma = jax.nn.sigmoid(pre)
    active = (pre * sigma).astype(jnp.bfloat16)
    back = dot(flat_g, down_matrix, ((1,), (1,)))
    pre_grad = (back * sigma * (1.0 + pre * (1.0 - sigma))).astype(jnp.bfloat16)
    row_grad = dot(pre_grad, up_matrix, ((1,), (1,))).astype(jnp.bfloat16)

    token_grad = pl.pallas_call(
        functools.partial(return_kernel, outer, inner),
        out_shape=jax.ShapeDtypeStruct((rows, width), jnp.bfloat16),
        in_specs=[any_space, vmem],
        out_specs=vmem,
        scratch_shapes=[
            pltpu.VMEM((CHUNKS, slots, wide), jnp.bfloat16),
            pltpu.VMEM((CHUNKS, outer * rows, wide), jnp.bfloat16),
            pltpu.VMEM((CHUNKS, outer * rows, wide), jnp.bfloat16),
            pltpu.VMEM((CHUNKS, rows, wide), jnp.float32),
            dma((CHUNKS, inner)), dma((CHUNKS, inner)),
            dma((CHUNKS, outer)), dma((CHUNKS, outer)),
        ],
        compiler_params=pltpu.CompilerParams(
            collective_id=1, has_side_effects=True, vmem_limit_bytes=48 * MIB
        ),
        name="bring_back",
    )(row_grad, put)

    up_grad = lax.psum_scatter(
        dot(flat_x, pre_grad, ((0,), (0,))).astype(jnp.bfloat16), "dp", scatter_dimension=0, tiled=True
    ).astype(jnp.float32)
    down_grad = lax.psum_scatter(
        dot(active, flat_g, ((0,), (0,))).astype(jnp.bfloat16), "dp", scatter_dimension=0, tiled=True
    ).astype(jnp.float32)
    return (token_grad, up_grad[None], down_grad[None])


def solution(mesh):
    in_specs = (
        P(("dp", "expert"), None),
        P(("dp", "expert"), None),
        P(("dp", "expert"), None),
        P(("dp", "expert"), None),
        P("expert", None, None),
        P("expert", None, None),
    )
    out_specs = (P(("dp", "expert"), None), P("expert", "dp", None), P("expert", "dp", None))
    return jax.shard_map(body, mesh=mesh, in_specs=in_specs, out_specs=out_specs, check_vma=False)
```
